32 devices in a mesh: row: 8 (over z, x), col: 4 (over y, core).
Axes of the slice: x: 2, y: 2, z: 4, core: 2. Of those that a mesh axis runs over, the one named last changes fastest.
Arguments:
- eigvecs: float32 [2048, 65536], P(('col', 'row')), may hold values from -6 to 6
- reflectors: float32 [4, 256, 65536], P(None, 'col', 'row'), may hold values from -0.0234375 to 0.0234375
- tfactors: float32 [4, 256, 256], replicated, may hold values from -0.5 to 2, as said below
Outputs:
- backed: float32 [65536, 2048], P('row', 'col')
The draws below stay inside these ranges and needn't reach their ends.
Inputs may be any that keep to these rules, and one draw needn't show every extreme that they name: `tfactors`: each block's factor is upper triangular with diagonal entries between 1 and 2.
All inputs are finite; a program needn't handle non-finite values.
Results may differ from the reference program's by a relative error of at most 0.0001.
Values sent between devices are 32-bit elements; how exact they have to be, the bound alone decides.
A program may use at most 128 MiB of HBM per device.

```python
import jax
import jax.numpy as jnp
from jax import lax

N = 65536
NB = 256
NBLK = 4
K = 2048


def draw_tfactors(key, part):
    first, second = jax.random.split(jax.random.fold_in(key, 11))
    shape = (NBLK, NB, NB)
    rows = lax.broadcasted_iota(jnp.int32, shape, 1)
    cols = lax.broadcasted_iota(jnp.int32, shape, 2)
    upper = jnp.clip(0.1 * jax.random.normal(first, shape, jnp.float32), -0.5, 0.5)
    diagon = jax.random.uniform(second, shape, jnp.float32, 1.0, 2.0)
    zeros = jnp.zeros(shape, jnp.float32)
    return jnp.where(cols > rows, upper, jnp.where(cols == rows, diagon, zeros))


def levels(own_key, extent, pieces, low, high):
    gain = 1.0
    for dim, shards_of in pieces:
        steps = jax.random.uniform(jax.random.fold_in(jax.random.fold_in(own_key, 6), dim), (shards_of,), jnp.float32, low / len(pieces), high / len(pieces))
        gain = gain * jnp.repeat(jnp.exp(steps), extent[dim] // shards_of).reshape((-1,) + (1,) * (len(extent) - 1 - dim))
    return gain


def normal_values(key, extent, spread, most, pieces=(), held_as=jnp.bfloat16):
    drawn = jax.random.normal(key, extent, jnp.float32) * spread
    if len(pieces) > 0:
        drawn = levels(key, extent, pieces, -0.22, 0.18) * drawn
    return jnp.clip(drawn, min=-most, max=most).astype(held_as)


def setup_inputs(seed: int = 0) -> dict:
    streams_of = jax.random.split(jax.random.key(seed), 4)
    eigvecs = normal_values(streams_of[0], (K, N), 1.0, 6.0, ((0, 32),), jnp.float32)
    reflectors = normal_values(streams_of[1], (NBLK, NB, N), N ** -0.5, 0.0234375, ((1, 4), (2, 8)), jnp.float32)
    tfactors = draw_tfactors(jax.random.fold_in(streams_of[3], 71), 0)
    return dict(eigvecs=eigvecs, reflectors=reflectors, tfactors=tfactors)


def matmul(left, right):
    return jnp.dot(left, right, precision=lax.Precision.HIGHEST, preferred_element_type=jnp.float32)


def reference(eigvecs, reflectors, tfactors):
    current = eigvecs.T
    for block in range(NBLK - 1, -1, -1):
        vectors = reflectors[block].T
        inner = matmul(vectors.T, current)
        scaled = matmul(tfactors[block], inner)
        current = current - matmul(vectors, scaled)
    return current
```

```python
import functools

import jax
import jax.numpy as jnp
from jax import lax
from jax.experimental import pallas as pl
from jax.experimental.pallas import tpu as pltpu
from jax.sharding import PartitionSpec as P

MESH = pl.DeviceIdType.MESH
PARTS = 4
TILE = 512


def split(value):
    high = value.astype(jnp.bfloat16)
    low = (value - high.astype(jnp.float32)).astype(jnp.bfloat16)
    return high, low


def product(left, right, dims):
    def one(a, b):
        return lax.dot_general(a, b, (dims, ((), ())), preferred_element_type=jnp.float32)

    return one(left[0], right[0]) + (one(left[0], right[1]) + one(left[1], right[0]))


def exact(left, right):
    return jnp.dot(left, right, precision=lax.Precision.HIGHEST, preferred_element_type=jnp.float32)


def allreduce(total, landed, full, send_sems, recv_sems, me, count):
    size = total.shape[0]
    offset = 0
    at = 0
    steps = []
    bit = 1
    index = 0
    while bit < count:
        size //= 2
        mine = lax.rem(me // bit, 2)
        partner = me + bit - 2 * bit * mine
        keep = pl.multiple_of(offset + mine * size, 8)
        give = pl.multiple_of(offset + (1 - mine) * size, 8)
        copy = pltpu.make_async_remote_copy(
            src_ref=total.at[pl.ds(give, size)],
            dst_ref=landed.at[pl.ds(at, size)],
            send_sem=send_sems.at[index],
            recv_sem=recv_sems.at[index],
            device_id={"row": partner},
            device_id_type=MESH,
        )
        copy.start()
        copy.wait()
        total[pl.ds(keep, size)] += landed[pl.ds(at, size)]
        steps.append((partner, keep, size))
        at += size
        offset = keep
        bit *= 2
        index += 1
    partner, keep, size = steps[-1]
    full[pl.ds(keep, size)] = total[pl.ds(keep, size)]
    for partner, keep, size in reversed(steps):
        piece = full.at[pl.ds(keep, size)]
        copy = pltpu.make_async_remote_copy(
            src_ref=piece,
            dst_ref=piece,
            send_sem=send_sems.at[index],
            recv_sem=recv_sems.at[index],
            device_id={"row": partner},
            device_id_type=MESH,
        )
        copy.start()
        copy.wait()
        index += 1


def kernel(
    shapes, eig, refl, tf, out, arrived, vec, gram, gram_in, gram_full, inner, inner_in, inner_full,
    scaled, scaled_hi, scaled_lo, x_send, x_recv, v_send, v_recv, r_send, r_recv, local,
):
    rows_n, cols_n = shapes
    row, col = lax.axis_index("row"), lax.axis_index("col")
    own, length = eig.shape[0], eig.shape[1] // rows_n
    blocks, _, share, _ = vec.shape
    nb = share * cols_n
    width = blocks * nb
    pairs = cols_n // 2
    core, place = lax.rem(col, 2), col // 2
    sibling = col + 1 - 2 * core
    step = own // PARTS
    nt = ((1,), (1,))

    barrier = pltpu.get_barrier_semaphore()
    for d in range(1, rows_n):
        pl.semaphore_signal(barrier, inc=1, device_id={"row": lax.rem(row + d, rows_n)}, device_id_type=MESH)
    for d in range(1, pairs):
        pl.semaphore_signal(barrier, inc=1, device_id={"col": lax.rem(place + d, pairs) * 2 + core}, device_id_type=MESH)
    pl.semaphore_signal(barrier, inc=1, device_id={"col": sibling}, device_id_type=MESH)
    pl.semaphore_wait(barrier, rows_n - 1 + pairs)

    def v_copy(src, slot, block, kind, target):
        copy = pltpu.make_async_remote_copy(
            src_ref=src,
            dst_ref=vec.at[block, slot],
            send_sem=v_send.at[block, kind],
            recv_sem=v_recv.at[block, kind],
            device_id={"col": target},
            device_id_type=MESH,
        )
        copy.start()
        return copy

    def x_start(part):
        copies = []
        for d in range(1, rows_n):
            target = lax.rem(row + d, rows_n)
            copy = pltpu.make_async_remote_copy(
                src_ref=eig.at[pl.ds(part * step, step), pl.ds(pl.multiple_of(target * length, 128), length)],
                dst_ref=arrived.at[row, pl.ds(part * step, step)],
                send_sem=x_send.at[part, d],
                recv_sem=x_recv.at[part, d],
                device_id={"row": target},
                device_id_type=MESH,
            )
            copy.start()
            copies.append(copy)
        return copies

    v_copies = []
    for b in range(blocks):
        direct = [v_copy(refl.at[b], col, b, d, lax.rem(place + d, pairs) * 2 + core) for d in range(1, pairs)]
        v_copies.append(direct)
    x_copies = [x_start(0), x_start(1)] + [None] * (PARTS - 2)
    near = [v_copy(refl.at[b], col, b, 0, sibling) for b in range(blocks)]
    v_local = pltpu.make_async_copy(refl, vec.at[:, col], local.at[0])
    v_local.start()
    x_local = pltpu.make_async_copy(
        eig.at[:, pl.ds(pl.multiple_of(row * length, 128), length)], arrived.at[row], local.at[1]
    )
    x_local.start()

    forwards = []
    for b in range(blocks):
        for d in range(1, pairs):
            v_copies[b][d - 1].wait_recv()
            slot = lax.rem(place + pairs - d, pairs) * 2 + core
            forwards.append(v_copy(vec.at[b, slot], slot, b, pairs + d - 1, sibling))
        if b == 1:
            x_copies[2] = x_start(2)
        if b == blocks - 1:
            x_copies[3] = x_start(3)
    v_local.wait()
    for copy in near + forwards:
        copy.wait()
    for direct in v_copies:
        for copy in direct:
            copy.wait_send()

    def vectors(start):
        tile = vec[:, :, :, pl.ds(pl.multiple_of(start, TILE), TILE)]
        return split(tile.reshape(width, TILE))

    gram[...] = jnp.zeros_like(gram)

    @pl.loop(0, length // TILE)
    def _(t):
        high, low = vectors(t * TILE)
        at = 0
        for i in range(blocks - 1):
            left = (high[i * nb : (i + 1) * nb], low[i * nb : (i + 1) * nb])
            for j in range(i + 1, blocks):
                right = (high[j * nb : (j + 1) * nb], low[j * nb : (j + 1) * nb])
                gram[pl.ds(at, nb)] += product(left, right, nt)
                at += nb

    allreduce(gram, gram_in, gram_full, r_send.at[PARTS], r_recv.at[PARTS], row, rows_n)
    x_local.wait()

    for part in range(PARTS):
        for copy in x_copies[part]:
            copy.wait()
        inner[...] = jnp.zeros_like(inner)


        def add_inner(x_ref):
            t = pl.program_id(0)
            piece = split(x_ref[...].reshape(rows_n * step, TILE))
            inner[...] += product(vectors(t * TILE), piece, nt)

        pltpu.emit_pipeline(
            add_inner,
            grid=(length // TILE,),
            in_specs=[pl.BlockSpec((rows_n, step, TILE), lambda t: (0, 0, t))],
            out_specs=[],
        )(arrived.at[:, pl.ds(part * step, step), :])
        allreduce(inner, inner_in, inner_full, r_send.at[part], r_recv.at[part], row, rows_n)
        found = [None] * blocks
        at = len(range(blocks)) * (blocks - 1) // 2 * nb
        for i in range(blocks - 1, -1, -1):
            term = inner_full[pl.ds(i * nb, nb)]
            at -= (blocks - 1 - i) * nb
            for j in range(i + 1, blocks):
                term = term - exact(gram_full[pl.ds(at + (j - i - 1) * nb, nb)], found[j])
            found[i] = exact(tf[i], term)
            scaled[:, pl.ds(part * step, step), pl.ds(i * nb, nb)] = found[i].T.reshape(rows_n, step, nb)

    high, low = split(scaled[...].reshape(rows_n * own, width))
    scaled_hi[...] = high
    scaled_lo[...] = low

    def finish(x_ref, out_ref):
        t = pl.program_id(0)
        change = product((scaled_hi[...], scaled_lo[...]), vectors(t * TILE), ((1,), (0,)))
        out_ref[...] = (x_ref[...].reshape(rows_n * own, TILE) - change).T

    pltpu.emit_pipeline(
        finish,
        grid=(length // TILE,),
        in_specs=[pl.BlockSpec((rows_n, own, TILE), lambda t: (0, 0, t))],
        out_specs=[pl.BlockSpec((TILE, rows_n * own), lambda t: (t, 0))],
    )(arrived, out)


def body(rows_n, cols_n, eigvecs, reflectors, tfactors):
    own, total = eigvecs.shape
    length = total // rows_n
    blocks, share, _ = reflectors.shape
    nb = share * cols_n
    width = blocks * nb
    wide = rows_n * own // PARTS
    grams = blocks * (blocks - 1) // 2 * nb
    steps = 2 * (rows_n.bit_length() - 1)
    f32, bf16 = jnp.float32, jnp.bfloat16
    hbm = pl.BlockSpec(memory_space=pl.ANY)
    result, _ = pl.pallas_call(
        functools.partial(kernel, (rows_n, cols_n)),
        out_shape=[
            jax.ShapeDtypeStruct((length, rows_n * own), f32),
            jax.ShapeDtypeStruct((rows_n, own, length), f32),
        ],
        in_specs=[hbm, hbm, pl.BlockSpec(memory_space=pltpu.VMEM)],
        out_specs=[hbm, hbm],
        scratch_shapes=[
            pltpu.VMEM((blocks, cols_n, share, length), f32),
            pltpu.VMEM((grams, nb), f32),
            pltpu.VMEM((grams, nb), f32),
            pltpu.VMEM((grams, nb), f32),
            pltpu.VMEM((width, wide), f32),
            pltpu.VMEM((width, wide), f32),
            pltpu.VMEM((width, wide), f32),
            pltpu.VMEM((rows_n, own, width), f32),
            pltpu.VMEM((rows_n * own, width), bf16),
            pltpu.VMEM((rows_n * own, width), bf16),
            pltpu.SemaphoreType.DMA((PARTS, rows_n)),
            pltpu.SemaphoreType.DMA((PARTS, rows_n)),
            pltpu.SemaphoreType.DMA((blocks, cols_n)),
            pltpu.SemaphoreType.DMA((blocks, cols_n)),
            pltpu.SemaphoreType.DMA((PARTS + 1, steps)),
            pltpu.SemaphoreType.DMA((PARTS + 1, steps)),
            pltpu.SemaphoreType.DMA((2,)),
        ],
        compiler_params=pltpu.CompilerParams(
            collective_id=0, has_side_effects=True, vmem_limit_bytes=60 * 1024 * 1024
        ),
    )(eigvecs, reflectors, tfactors)
    return result


def solution(mesh):
    in_specs = (P(("col", "row"), None), P(None, "col", "row"), P())
    out_specs = P("row", "col")
    part = functools.partial(body, mesh.shape["row"], mesh.shape["col"])
    return jax.shard_map(part, mesh=mesh, in_specs=in_specs, out_specs=out_specs, check_vma=False)
```

```python
import functools

import jax
import jax.numpy as jnp
from jax import lax
from jax.experimental import pallas as pl
from jax.experimental.pallas import tpu as pltpu
from jax.sharding import PartitionSpec as P

MESH = pl.DeviceIdType.MESH
PARTS = 4
TILE = 512


def split(value):
    high = value.astype(jnp.bfloat16)
    low = (value - high.astype(jnp.float32)).astype(jnp.bfloat16)
    return high, low


def product(left, right, dims):
    def one(a, b):
        return lax.dot_general(a, b, (dims, ((), ())), preferred_element_type=jnp.float32)

    return one(left[0], right[0]) + (one(left[0], right[1]) + one(left[1], right[0]))


def exact(left, right):
    return jnp.dot(left, right, precision=lax.Precision.HIGHEST, preferred_element_type=jnp.float32)


def allreduce(total, landed, full, send_sems, recv_sems, me, count):
    size = total.shape[0]
    offset = 0
    at = 0
    steps = []
    bit = 1
    index = 0
    while bit < count:
        size //= 2
        mine = lax.rem(me // bit, 2)
        partner = me + bit - 2 * bit * mine
        keep = pl.multiple_of(offset + mine * size, 8)
        give = pl.multiple_of(offset + (1 - mine) * size, 8)
        copy = pltpu.make_async_remote_copy(
            src_ref=total.at[pl.ds(give, size)],
            dst_ref=landed.at[pl.ds(at, size)],
            send_sem=send_sems.at[index],
            recv_sem=recv_sems.at[index],
            device_id={"row": partner},
            device_id_type=MESH,
        )
        copy.start()
        yield
        copy.wait()
        total[pl.ds(keep, size)] += landed[pl.ds(at, size)]
        steps.append((partner, keep, size))
        at += size
        offset = keep
        bit *= 2
        index += 1
    partner, keep, size = steps[-1]
    full[pl.ds(keep, size)] = total[pl.ds(keep, size)]
    for partner, keep, size in reversed(steps):
        piece = full.at[pl.ds(keep, size)]
        copy = pltpu.make_async_remote_copy(
            src_ref=piece,
            dst_ref=piece,
            send_sem=send_sems.at[index],
            recv_sem=recv_sems.at[index],
            device_id={"row": partner},
            device_id_type=MESH,
        )
        copy.start()
        yield
        copy.wait()
        index += 1


def kernel(
    shapes, eig, refl, tf, out, arrived, vec, gram, gram_in, gram_full, held, inner, inner_in, inner_full,
    scaled, scaled_hi, scaled_lo, x_send, x_recv, v_send, v_recv, r_send, r_recv, local,
):
    rows_n, cols_n = shapes
    row, col = lax.axis_index("row"), lax.axis_index("col")
    own, length = eig.shape[0], eig.shape[1] // rows_n
    blocks, _, share, _ = vec.shape
    nb = share * cols_n
    width = blocks * nb
    pairs = cols_n // 2
    core, place = lax.rem(col, 2), col // 2
    sibling = col + 1 - 2 * core
    step = own // PARTS
    nt = ((1,), (1,))

    barrier = pltpu.get_barrier_semaphore()
    for d in range(1, rows_n):
        pl.semaphore_signal(barrier, inc=1, device_id={"row": lax.rem(row + d, rows_n)}, device_id_type=MESH)
    for d in range(1, pairs):
        pl.semaphore_signal(barrier, inc=1, device_id={"col": lax.rem(place + d, pairs) * 2 + core}, device_id_type=MESH)
    pl.semaphore_signal(barrier, inc=1, device_id={"col": sibling}, device_id_type=MESH)
    pl.semaphore_wait(barrier, rows_n - 1 + pairs)

    def v_copy(src, slot, block, kind, target):
        copy = pltpu.make_async_remote_copy(
            src_ref=src,
            dst_ref=vec.at[block, slot],
            send_sem=v_send.at[block, kind],
            recv_sem=v_recv.at[block, kind],
            device_id={"col": target},
            device_id_type=MESH,
        )
        copy.start()
        return copy

    def x_start(part):
        copies = []
        for d in sorted(range(1, rows_n), key=lambda d: abs(2 * d - rows_n)):
            target = lax.rem(row + d, rows_n)
            copy = pltpu.make_async_remote_copy(
                src_ref=eig.at[pl.ds(part * step, step), pl.ds(pl.multiple_of(target * length, 128), length)],
                dst_ref=arrived.at[row, pl.ds(part * step, step)],
                send_sem=x_send.at[part, d],
                recv_sem=x_recv.at[part, d],
                device_id={"row": target},
                device_id_type=MESH,
            )
            copy.start()
            copies.append(copy)
        return copies

    v_copies = []
    for b in range(blocks):
        direct = [v_copy(refl.at[b], col, b, d, lax.rem(place + d, pairs) * 2 + core) for d in range(1, pairs)]
        v_copies.append(direct)
    x_copies = [x_start(0), x_start(1), x_start(2), None]
    near = [v_copy(refl.at[b], col, b, 0, sibling) for b in range(blocks)]
    v_local = pltpu.make_async_copy(refl, vec.at[:, col], local.at[0])
    v_local.start()
    x_local = pltpu.make_async_copy(
        eig.at[:, pl.ds(pl.multiple_of(row * length, 128), length)], arrived.at[row], local.at[1]
    )
    x_local.start()

    v_local.wait()
    gram[...] = jnp.zeros_like(gram)

    def vectors(start, first=0, last=blocks):
        tile = vec[first:last, :, :, pl.ds(pl.multiple_of(start, TILE), TILE)]
        return split(tile.reshape((last - first) * nb, TILE))

    def pair(i, j):
        return (i * (2 * blocks - 1 - i) // 2 + j - i - 1) * nb

    for b in range(blocks):
        forwards = []
        for d in range(1, pairs):
            v_copies[b][d - 1].wait_recv()
            slot = lax.rem(place + pairs - d, pairs) * 2 + core
            forwards.append(v_copy(vec.at[b, slot], slot, b, pairs + d - 1, sibling))
        if b == 1:
            x_copies[3] = x_start(3)
        near[b].wait()
        for copy in forwards:
            copy.wait()
        if b > 0:

            @pl.loop(0, length // TILE)
            def _(t):
                left = vectors(t * TILE, 0, b)
                found = product(left, vectors(t * TILE, b, b + 1), nt)
                for i in range(b):
                    gram[pl.ds(pair(i, b), nb)] += found[i * nb : (i + 1) * nb]

    for direct in v_copies:
        for copy in direct:
            copy.wait_send()

    def solve(part):
        found = [None] * blocks
        for i in range(blocks - 1, -1, -1):
            term = inner_full[pl.ds(i * nb, nb)]
            for j in range(i + 1, blocks):
                term = term - exact(gram_full[pl.ds(pair(i, j), nb)], found[j])
            found[i] = exact(tf[i], term)
            scaled[:, pl.ds(part * step, step), pl.ds(i * nb, nb)] = found[i].T.reshape(rows_n, step, nb)

    tiles = length // TILE
    stops = 2 * (rows_n.bit_length() - 1)
    x_local.wait()
    pending = allreduce(gram, gram_in, gram_full, r_send.at[PARTS], r_recv.at[PARTS], row, rows_n)
    next(pending)
    for part in range(PARTS):
        if part >= 2:
            for _ in pending:
                pass
            solve(part - 1)
        for copy in x_copies[part]:
            copy.wait()
        load = pltpu.make_async_copy(arrived.at[:, pl.ds(part * step, step), :], held, local.at[2])
        load.start()
        total = inner.at[part % 2]
        total[...] = jnp.zeros_like(total)
        load.wait()
        for stop in range(stops):

            @pl.loop(tiles * stop // stops, tiles * (stop + 1) // stops)
            def _(t):
                start = pl.multiple_of(t * TILE, TILE)
                piece = split(held[:, :, pl.ds(start, TILE)].reshape(rows_n * step, TILE))
                total[...] += product(vectors(start), piece, nt)

            next(pending, None)
        for _ in pending:
            pass
        if part == 1:
            solve(0)
        pending = allreduce(total, inner_in, inner_full, r_send.at[part], r_recv.at[part], row, rows_n)
        next(pending)
    for _ in pending:
        pass
    solve(PARTS - 1)

    high, low = split(scaled[...].reshape(rows_n * own, width))
    scaled_hi[...] = high
    scaled_lo[...] = low

    def finish(x_ref, out_ref):
        t = pl.program_id(0)
        change = product((scaled_hi[...], scaled_lo[...]), vectors(t * TILE), ((1,), (0,)))
        out_ref[...] = (x_ref[...].reshape(rows_n * own, TILE) - change).T

    pltpu.emit_pipeline(
        finish,
        grid=(length // TILE,),
        in_specs=[pl.BlockSpec((rows_n, own, TILE), lambda t: (0, 0, t))],
        out_specs=[pl.BlockSpec((TILE, rows_n * own), lambda t: (t, 0))],
    )(arrived, out)


def body(rows_n, cols_n, eigvecs, reflectors, tfactors):
    own, total = eigvecs.shape
    length = total // rows_n
    blocks, share, _ = reflectors.shape
    nb = share * cols_n
    width = blocks * nb
    wide = rows_n * own // PARTS
    grams = blocks * (blocks - 1) // 2 * nb
    steps = 2 * (rows_n.bit_length() - 1)
    f32, bf16 = jnp.float32, jnp.bfloat16
    hbm = pl.BlockSpec(memory_space=pl.ANY)
    result, _ = pl.pallas_call(
        functools.partial(kernel, (rows_n, cols_n)),
        out_shape=[
            jax.ShapeDtypeStruct((length, rows_n * own), f32),
            jax.ShapeDtypeStruct((rows_n, own, length), f32),
        ],
        in_specs=[hbm, hbm, pl.BlockSpec(memory_space=pltpu.VMEM)],
        out_specs=[hbm, hbm],
        scratch_shapes=[
            pltpu.VMEM((blocks, cols_n, share, length), f32),
            pltpu.VMEM((grams, nb), f32),
            pltpu.VMEM((grams, nb), f32),
            pltpu.VMEM((grams, nb), f32),
            pltpu.VMEM((rows_n, own // PARTS, length), f32),
            pltpu.VMEM((2, width, wide), f32),
            pltpu.VMEM((width, wide), f32),
            pltpu.VMEM((width, wide), f32),
            pltpu.VMEM((rows_n, own, width), f32),
            pltpu.VMEM((rows_n * own, width), bf16),
            pltpu.VMEM((rows_n * own, width), bf16),
            pltpu.SemaphoreType.DMA((PARTS, rows_n)),
            pltpu.SemaphoreType.DMA((PARTS, rows_n)),
            pltpu.SemaphoreType.DMA((blocks, cols_n)),
            pltpu.SemaphoreType.DMA((blocks, cols_n)),
            pltpu.SemaphoreType.DMA((PARTS + 1, steps)),
            pltpu.SemaphoreType.DMA((PARTS + 1, steps)),
            pltpu.SemaphoreType.DMA((3,)),
        ],
        compiler_params=pltpu.CompilerParams(
            collective_id=0, has_side_effects=True, vmem_limit_bytes=60 * 1024 * 1024
        ),
    )(eigvecs, reflectors, tfactors)
    return result


def solution(mesh):
    in_specs = (P(("col", "row"), None), P(None, "col", "row"), P())
    out_specs = P("row", "col")
    part = functools.partial(body, mesh.shape["row"], mesh.shape["col"])
    return jax.shard_map(part, mesh=mesh, in_specs=in_specs, out_specs=out_specs, check_vma=False)
```
